256 devices in a mesh: row: 16 (over y, x_lo, core), col: 16 (over z, x_hi).
Axes of the slice: x: 4 (x_hi: 2, x_lo: 2; x = x_hi * 2 + x_lo), y: 4, z: 8, core: 2. Of those that a mesh axis runs over, the one named last changes fastest.
Arguments:
- inverse_rows: float32 [16384, 16384], P('col', 'row'), may hold values from -0.5 to 0.5
- panels: float32 [16, 16384, 256], P('col', 'row'), may hold values from -0.75 to 0.75
- diag_inverse: float32 [2, 256, 256], replicated, may hold values from -12 to 12
- pattern: int32 [2, 64], replicated, may hold values 0 or 1
- owner_slot: int32 [2], replicated, may hold values from 0 to 15, as said below
Outputs:
- inverse_column: float32 [2, 16384, 256], P(None, 'row')
- inverse_row: float32 [2, 256, 16384], P(None, None, 'col')
- diag_block: float32 [2, 256, 256], replicated
The draws below stay inside these ranges and needn't reach their ends.
Inputs may be any that keep to these rules, and one draw needn't show every extreme that they name: `owner_slot`: the two supernodes' panels lie in two different slots, one of them the last slot.
All inputs are finite; a program needn't handle non-finite values.
Results may differ from the reference program's by a relative error of at most 0.0001.
Values sent between devices are 32-bit elements; how exact they have to be, the bound alone decides.
No kernel may reach another device: no remote copies, remote signals or barrier semaphores. Data moves between devices by JAX's collectives and lax.ppermute only.
A program may use at most 64 MiB of HBM per device.

```python
import jax
import jax.numpy as jnp
from jax import lax

W = 256
BLOCKS = 64
M = 16384
SLOTS = 16


def draw_owner_slot(key, part):
    first_key = jax.random.fold_in(key, 11)
    second_key = jax.random.fold_in(key, 23)
    other = jax.random.randint(first_key, (), 0, SLOTS - 1).astype(jnp.int32)
    flip = jax.random.randint(second_key, (), 0, 2).astype(jnp.int32)
    last = jnp.int32(SLOTS - 1)
    return jnp.where(flip == 1, jnp.stack([last, other]), jnp.stack([other, last])).astype(jnp.int32)


def touch_ends(result, stream_key, least, high):
    dims = result.shape
    index_at = [jax.random.randint(jax.random.fold_in(stream_key, axis), (), 0, dims[axis]) for axis in range(len(dims))]
    result = result.at[tuple(index_at)].set(least)
    longest = dims.index(max(dims))
    index_at[longest] = (index_at[longest] + 1) % dims[longest]
    return result.at[tuple(index_at)].set(high)


def raised(values, key, source, target, blocks, factor):
    owner, partner = [(jnp.arange(values.shape[dim]) // (values.shape[dim] // blocks)).reshape([-1 if axis == dim else 1 for axis in range(values.ndim)]) for dim in (source, target)]
    chosen = jax.random.permutation(key, blocks)[partner]
    strong = (owner == chosen) | (owner == (partner + blocks // 2) % blocks)
    return jnp.where(strong, factor * values, values)


def block_levels(key, shape, shards, smallest, largest):
    factor_of, own = 1.0, jax.random.fold_in(key, 6)
    for dim, shards_of in shards:
        draws = jnp.exp(jax.random.uniform(jax.random.fold_in(own, dim), (shards_of,), jnp.float32, smallest / len(shards), largest / len(shards)))
        factor_of = factor_of * jnp.repeat(draws, shape[dim] // shards_of).reshape([-1 if axis == dim else 1 for axis in range(len(shape))])
    return factor_of


def bell_draw(own_key, extent, scale, reach, shards=(), dtype=jnp.bfloat16):
    array = scale * jax.random.normal(own_key, extent, jnp.float32)
    if shards:
        array = array * block_levels(own_key, extent, shards, -0.22, 0.18)
    return jnp.clip(array, -reach, reach).astype(dtype)


def bell_draw_with(own_key, shape, scale, limit, cuts, heavy, dtype=jnp.bfloat16):
    values = scale * jax.random.normal(own_key, shape, jnp.float32)
    if cuts:
        values = values * block_levels(own_key, shape, cuts, -0.22, 0.18)
    return jnp.clip(raised(values, jax.random.fold_in(own_key, 3), *heavy), -limit, limit).astype(dtype)


def setup_inputs(seed: int = 0) -> dict:
    keys = jax.random.split(jax.random.key(seed), 6)
    return {
        "inverse_rows": bell_draw_with(keys[0], (M, M), (M // 64) ** -0.5, 0.5, ((0, 16), (1, 16)), (1, 0, 16, 2.0), jnp.float32),
        "panels": bell_draw(keys[1], (SLOTS, M, W), 0.125, 0.75, ((0, 16), (1, 16)), jnp.float32),
        "diag_inverse": bell_draw(keys[2], (2, W, W), 2.0, 12.0, (), jnp.float32),
        "pattern": touch_ends((jax.random.randint(keys[3], (2, BLOCKS), 0, 3) < 2).astype(jnp.int32), jax.random.fold_in(keys[3], 1), 0, 1),
        "owner_slot": draw_owner_slot(jax.random.fold_in(keys[5], 71), 0),
    }


def reference(inverse_rows, panels, diag_inverse, pattern, owner_slot):
    columns = []
    transposed = []
    diagonals = []
    for number in range(2):
        rowmask = jnp.repeat(pattern[number].astype(jnp.float32), W)
        chosen = lax.dynamic_index_in_dim(panels, owner_slot[number].astype(jnp.int32), 0, keepdims=False)
        masked = rowmask[:, None] * chosen
        product = jnp.dot(inverse_rows, masked, precision=lax.Precision.HIGHEST, preferred_element_type=jnp.float32)
        column = -(rowmask[:, None] * product)
        columns.append(column)
        transposed.append(column.T)
        inner = jnp.dot(masked.T, column, precision=lax.Precision.HIGHEST, preferred_element_type=jnp.float32)
        diagonals.append(diag_inverse[number] - inner)
    return jnp.stack(columns), jnp.stack(transposed), jnp.stack(diagonals)
```

```python
import jax
import jax.numpy as jnp
import numpy as np
from jax import lax
from jax.sharding import Mesh
from jax.sharding import PartitionSpec as P

SIZES = {"y": 4, "xl": 2, "core": 2, "z": 8, "xh": 2}
ROW = ("y", "xl", "core")
CHIP = ("y", "xl")
COL = ("z", "xh")
ALL = ROW + COL


def swap_pairs():
    return [(0, 1), (1, 0)]


def turn_pairs(step):
    n = SIZES["z"]
    return [(i, (i + step) % n) for i in range(n)]


def transpose_pairs():
    return [(r * 16 + c, c * 16 + r) for r in range(16) for c in range(16)]


def both(mine, other, first):
    return jnp.where(first, jnp.stack([mine, other]), jnp.stack([other, mine]))


def ring(block, axis_dim):
    z = lax.axis_index("z")
    n = SIZES["z"]
    half = block.shape[-2] // 2
    shape = block.shape[:axis_dim] + (n,) + block.shape[axis_dim:]
    out = jnp.zeros(shape, block.dtype)

    def put(out, piece, index, row):
        start = [0] * len(shape)
        start[axis_dim] = index % n
        start[-2] = row
        return lax.dynamic_update_slice(out, jnp.expand_dims(piece, axis_dim), start)

    out = put(out, block, z, 0)
    up = down = block
    for k in range(1, 4):
        up = lax.ppermute(up, "z", turn_pairs(1))
        down = lax.ppermute(down, "z", turn_pairs(-1))
        out = put(out, up, z - k + n, 0)
        out = put(out, down, z + k, 0)
    up = lax.ppermute(up[..., :half, :], "z", turn_pairs(1))
    down = lax.ppermute(down[..., half:, :], "z", turn_pairs(-1))
    out = put(out, up, z + 4, 0)
    out = put(out, down, z + 4, half)
    return out


def dot(a, b):
    return jnp.dot(a, b, precision=lax.Precision.HIGH, preferred_element_type=jnp.float32)


def shards(inverse_rows, panels, diag_inverse, pattern, owner_slot):
    row = lax.axis_index(ROW)
    col = lax.axis_index(COL)
    chip = lax.axis_index(CHIP)
    core = lax.axis_index("core")
    xh = lax.axis_index("xh")
    live = pattern.astype(jnp.float32)

    dealt = lax.all_to_all(panels[0].reshape(16, 64, 256), COL, 0, 0, tiled=True)
    mask = lax.dynamic_slice_in_dim(live, row * 4 + col // 4, 1, 1)[:, :, None]
    chunk = mask * jnp.stack(
        [lax.dynamic_index_in_dim(dealt, owner_slot[s], 0, keepdims=False) for s in range(2)]
    )
    chunk = jnp.concatenate([chunk[0], chunk[1]], axis=1)
    other = lax.ppermute(chunk, "xh", swap_pairs())
    block = both(chunk, other, xh == 0).reshape(128, 512)
    masked = ring(block, 0).reshape(1024, 512)

    first = core == 0
    send_in = jnp.where(first, masked[:, 256:], masked[:, :256])
    keep_in = jnp.where(first, masked[:, :256], masked[:, 256:])
    received = lax.ppermute(dot(inverse_rows, send_in), "core", swap_pairs())
    term = dot(inverse_rows, keep_in) + received
    terms = lax.all_to_all(term.reshape(8, 128, 256), CHIP, 0, 0, tiled=True)
    total = jnp.sum(terms, axis=0)
    mask = lax.dynamic_slice(live, (core, col * 4 + chip // 2), (1, 1))
    column = -(mask * total)

    rows = lax.all_gather(column.T, ROW, axis=0, tiled=False)
    rows = rows.reshape(8, 2, 256, 128).transpose(1, 2, 0, 3).reshape(2, 256, 1024)

    other = lax.ppermute(column, "core", swap_pairs())
    pair = both(column, other, first)
    pair = lax.ppermute(pair, ALL, transpose_pairs())
    lower = ring(pair, 1).reshape(2, 1024, 256)

    left = jnp.where(xh == 0, block[:, :256], block[:, 256:])
    right = jnp.where(xh == 0, pair[0], pair[1])
    inner = dot(left.T, right)
    inner = jnp.sum(lax.all_to_all(inner.reshape(16, 16, 256), ROW, 0, 0, tiled=True), axis=0)
    spread = jnp.broadcast_to(inner[None], (8, 16, 256))
    inner = jnp.sum(lax.all_to_all(spread, "z", 0, 0, tiled=True), axis=0)
    spread = jnp.broadcast_to(inner[None], (32, 16, 256))
    inner = lax.all_to_all(spread, ROW + ("xh",), 0, 0, tiled=True)
    inner = inner.reshape(16, 2, 16, 256).transpose(1, 0, 2, 3).reshape(2, 256, 256)
    return lower, rows, diag_inverse - inner


def solution(mesh):
    fine = Mesh(np.asarray(mesh.devices).reshape(4, 2, 2, 8, 2), ALL)
    in_specs = (P(COL, ROW), P(COL, ROW, None), P(), P(), P())
    out_specs = (P(None, ROW, None), P(None, None, COL), P())
    return jax.shard_map(shards, mesh=fine, in_specs=in_specs, out_specs=out_specs, check_vma=False)
```

```python
import functools

import jax
import jax.numpy as jnp
import numpy as np
from jax import lax
from jax.experimental import pallas as pl
from jax.experimental.pallas import tpu as pltpu
from jax.sharding import Mesh
from jax.sharding import PartitionSpec as P

ROW = ("y", "xl", "core")
CHIP = ("y", "xl")
COL = ("z", "xh")
ALL = ROW + COL
SMEM = pl.BlockSpec(memory_space=pltpu.SMEM)
VMEM = pl.BlockSpec(memory_space=pltpu.VMEM)
ANY = pl.BlockSpec(memory_space=pl.ANY)
SWAP = [(0, 1), (1, 0)]
TRANSPOSE = [(r * 16 + c, c * 16 + r) for r in range(16) for c in range(16)]
UP = [(i, (i + 1) % 8) for i in range(8)]
DOWN = [(i, (i - 1) % 8) for i in range(8)]


def call(kernel, outs, ins, outputs, flops=0, nbytes=1 << 21, scratch=(), mib=24, **rest):
    shapes = [jax.ShapeDtypeStruct(shape, dtype) for shape, dtype in outs]
    return pl.pallas_call(
        kernel,
        out_shape=shapes if len(shapes) > 1 else shapes[0],
        in_specs=ins,
        out_specs=outputs if len(shapes) > 1 else outputs[0],
        scratch_shapes=list(scratch),
        compiler_params=pltpu.CompilerParams(vmem_limit_bytes=mib << 20),
        cost_estimate=pl.CostEstimate(flops=flops, bytes_accessed=nbytes, transcendentals=0),
        **rest,
    )


def halves(value):
    high = value.astype(jnp.bfloat16)
    low = (value - high.astype(jnp.float32)).astype(jnp.bfloat16)
    return high, low


def dot3(left, right):
    dot = functools.partial(jnp.dot, preferred_element_type=jnp.float32)
    return dot(left[0], right[1]) + dot(left[1], right[0]) + dot(left[0], right[0])


def first_kernel(number, left, right, out, high, low, right_high, right_low):
    columns = pl.ds(pl.multiple_of(number[0] * 256, 256), 256)

    @pl.when(pl.program_id(0) == 0)
    def _():
        right_high[...], right_low[...] = halves(right[:, columns])

    pair = halves(left[...])
    high[...], low[...] = pair
    out[...] = dot3(pair, (right_high[...], right_low[...]))


def second_kernel(number, high, low, right, out, right_high, right_low):
    columns = pl.ds(pl.multiple_of(number[0] * 256, 256), 256)

    @pl.when(pl.program_id(0) == 0)
    def _():
        right_high[...], right_low[...] = halves(right[:, columns])

    out[...] = dot3((high[...], low[...]), (right_high[...], right_low[...]))


def product(number, left, right):
    block = pl.BlockSpec((256, 1024), lambda i: (i, 0))
    out_block = pl.BlockSpec((256, 256), lambda i: (i, 0))
    whole = pl.BlockSpec((1024, 512), lambda i: (0, 0))
    half = pltpu.VMEM((1024, 256), jnp.bfloat16)
    kept = ((1024, 1024), jnp.bfloat16)
    out = ((1024, 256), jnp.float32)
    rest = dict(flops=3 << 29, nbytes=7 << 20, scratch=[half, half], grid=(4,))
    if len(left) == 1:
        outs, specs = [out, kept, kept], [out_block, block, block]
        return call(first_kernel, outs, [SMEM, block, whole], specs, **rest)(number, *left, right)
    return call(second_kernel, [out], [SMEM, block, block, whole], [out_block], **rest)(number, *left, right)


def choose_kernel(at, *refs):
    *parts, out = refs
    for number in range(2):
        for k in range(8):

            @pl.when(at[number] == k)
            def _(number=number, k=k):
                out[number] = parts[k][...]


def block_kernel(slots, at, pattern, mine, other, out):
    for number in range(2):
        columns = slice(number * 256, number * 256 + 256)
        which = jnp.where(slots[number] == 15, 1, 0)
        mask = pattern[number, at[0]].astype(jnp.float32)
        absent = at[1 + which]

        @pl.when(absent == 0)
        def _():
            out[:, columns] = mask * mine[which]

        @pl.when(absent != 0)
        def _():
            out[:, columns] = mask * other[which]


def reduce_kernel(at, pattern, terms, column, spread):
    total = terms[0]
    for k in range(1, 8):
        total += terms[k]
    total = -(pattern[at[0], at[1]].astype(jnp.float32) * total)
    column[...] = total
    turned = total.T
    for k in range(8):
        spread[k] = turned


def inner_kernel(at, left, right, unused, out, same):
    rows = pl.ds(pl.multiple_of(at[0] * 128, 128), 128)
    columns = pl.ds(pl.multiple_of(at[1] * 256, 256), 256)
    inner = dot3(halves(left[rows, columns].T), halves(right[...]))
    for k in range(16):
        out[k] = inner[k * 16 : k * 16 + 16]
    same[...] = right[...]


def rows_kernel(core, mine, other, out):
    for k in range(8):
        columns = slice(k * 128, k * 128 + 128)
        out[core[0], :, columns] = mine[k]
        out[1 - core[0], :, columns] = other[k]


def diag_kernel(given, pieces, out):
    for number in range(2):
        for k in range(16):
            rows = slice(k * 16, k * 16 + 16)
            out[number, rows] = given[number, rows] - pieces[2 * k + number]


def pack_kernel(xh, mine, other, inner, out):
    out[pl.ds(pl.multiple_of(xh[0] * 144, 16), 128)] = mine[...]
    out[pl.ds(pl.multiple_of((1 - xh[0]) * 144, 16), 128)] = other[...]
    total = inner[0]
    for k in range(1, 16):
        total += inner[k]
    out[128:144] = total


def place_kernel(z, *refs):
    *pieces, top, bottom, out = refs
    for piece, index in zip(pieces, (0, 7, 6, 5, 1, 2, 3)):
        start = pl.multiple_of(lax.rem(z[0] + index, 8) * 128, 128)
        out[0, pl.ds(start, 128)] = piece[:128]
        out[1, pl.ds(start, 128)] = piece[144:]
    start = pl.multiple_of(lax.rem(z[0] + 4, 8) * 128, 128)
    out[0, pl.ds(start, 128)] = top[:128]
    out[1, pl.ds(start, 128)] = bottom[8:]


def both(mine, other, first):
    return jnp.where(first, jnp.stack([mine, other]), jnp.stack([other, mine]))


def ring(block):
    half = block.shape[-2] // 2
    ups, downs = [block], [block]
    for _ in range(3):
        ups.append(lax.ppermute(ups[-1], "z", UP))
        downs.append(lax.ppermute(downs[-1], "z", DOWN))
    top = lax.ppermute(ups[-1][..., :half, :], "z", UP)
    bottom = lax.ppermute(downs[-1][..., half:, :], "z", DOWN)
    return [block] + ups[1:] + downs[1:] + [top, bottom]


def deal(slot, parts):
    steps = [[(s, (s + 2 * k) % 16) for s in (slot, 15)] for k in range(1, 8)]
    return tuple(lax.ppermute(part, COL, pairs) for part, pairs in zip(parts, steps))


def gather_rows(pieces, z):
    out = jnp.zeros((1024, pieces[0].shape[1]), jnp.float32)
    index = [z, z + 7, z + 6, z + 5, z + 1, z + 2, z + 3, z + 4, z + 4]
    for k, piece in enumerate(pieces):
        out = lax.dynamic_update_slice(out, piece, (index[k] % 8 * 128 + (64 if k == 8 else 0), 0))
    return out


def shards(inverse_rows, panels, diag_inverse, pattern, owner_slot):
    row = lax.axis_index(ROW)
    col = lax.axis_index(COL)
    chip = lax.axis_index(CHIP)
    core = lax.axis_index("core")
    z = lax.axis_index("z")
    xh = lax.axis_index("xh")

    parts = panels[0].reshape(8, 128, 256)
    parts = [lax.dynamic_index_in_dim(parts, (z + k) % 8, 0, keepdims=False) for k in range(8)]
    least = jnp.min(owner_slot)
    arrived = lax.switch(least, [functools.partial(deal, slot) for slot in range(15)], tuple(parts[1:]))
    out = ((2, 128, 256), jnp.float32)
    at = jnp.stack([(z + 8 - least // 2) % 8, (z + 1) % 8])
    mine = call(choose_kernel, [out], [SMEM] + [VMEM] * 8, [VMEM], nbytes=1 << 20)(at, parts[0], *arrived)
    other = lax.ppermute(mine, "xh", SWAP)
    out = ((128, 512), jnp.float32)
    at = jnp.stack([row * 4 + z // 2, jnp.where(least % 2 == xh, 0, 1), 1 - xh])
    block = call(block_kernel, [out], [SMEM] * 3 + [VMEM] * 2, [VMEM], nbytes=1 << 19)(
        owner_slot, at, pattern, mine, other
    )
    masked = gather_rows(ring(block), z)

    sent, *kept = product((1 - core)[None], [inverse_rows], masked)
    received = lax.ppermute(sent, "core", SWAP)
    term = product(core[None], kept, masked) + received
    terms = lax.all_to_all(term.reshape(8, 128, 256), CHIP, 0, 0, tiled=True)
    outs = [((128, 256), jnp.float32), ((8, 256, 128), jnp.float32)]
    at = jnp.stack([core, col * 4 + chip // 2])
    column, spread = call(reduce_kernel, outs, [SMEM, SMEM, VMEM], [VMEM, VMEM])(at, pattern, terms)

    turned = lax.all_to_all(spread, CHIP, 0, 0, tiled=True)
    mine = lax.ppermute(column, ALL, TRANSPOSE)
    outs = [((16, 16, 256), jnp.float32), ((128, 256), jnp.float32)]
    at = jnp.stack([z, xh])
    inner, mine = call(inner_kernel, outs, [SMEM, VMEM, VMEM, ANY], [VMEM] * 2, flops=3 << 24)(at, masked, mine, turned)
    other = lax.ppermute(mine, "xh", SWAP)
    inner = lax.all_to_all(inner, ROW, 0, 0, tiled=True)

    out = ((272, 256), jnp.float32)
    block = call(pack_kernel, [out], [SMEM] + [VMEM] * 3, [VMEM])(xh[None], mine, other, inner)
    pieces = ring(block)
    out = ((2, 1024, 256), jnp.float32)
    lower = call(place_kernel, [out], [SMEM] + [VMEM] * 9, [VMEM], nbytes=1 << 22)(z[None], *pieces)

    last = jnp.concatenate([pieces[7][128:], pieces[8][:8]])
    inner = sum([piece[128:144] for piece in pieces[:7]], last)
    inner = jnp.broadcast_to(inner[None], (32, 16, 256))
    inner = lax.all_to_all(inner, ROW + ("xh",), 0, 0, tiled=True)
    out = ((2, 256, 256), jnp.float32)
    diag = call(diag_kernel, [out], [VMEM, VMEM], [VMEM], nbytes=3 << 19)(diag_inverse, inner)

    other = lax.ppermute(turned, "core", SWAP)
    out = ((2, 256, 1024), jnp.float32)
    rows = call(rows_kernel, [out], [SMEM, VMEM, VMEM], [VMEM], nbytes=1 << 22)(core[None], turned, other)
    return lower, rows, diag


def solution(mesh):
    fine = Mesh(np.asarray(mesh.devices).reshape(4, 2, 2, 8, 2), ALL)
    in_specs = (P(COL, ROW), P(COL, ROW, None), P(), P(), P())
    out_specs = (P(None, ROW, None), P(None, None, COL), P())
    return jax.shard_map(shards, mesh=fine, in_specs=in_specs, out_specs=out_specs, check_vma=False)
```

```python
import functools

import jax
import jax.numpy as jnp
import numpy as np
from jax import lax
from jax.experimental import pallas as pl
from jax.experimental.pallas import tpu as pltpu
from jax.sharding import Mesh
from jax.sharding import PartitionSpec as P

ROW = ("y", "xl", "core")
CHIP = ("y", "xl")
COL = ("z", "xh")
ALL = ROW + COL
SMEM = pl.BlockSpec(memory_space=pltpu.SMEM)
VMEM = pl.BlockSpec(memory_space=pltpu.VMEM)
ANY = pl.BlockSpec(memory_space=pl.ANY)
SWAP = [(0, 1), (1, 0)]
TRANSPOSE = [(r * 16 + c, c * 16 + r) for r in range(16) for c in range(16)]
UP = [(i, (i + 1) % 8) for i in range(8)]
DOWN = [(i, (i - 1) % 8) for i in range(8)]


def call(kernel, outs, ins, outputs, flops=0, nbytes=1 << 21, scratch=(), mib=24, **rest):
    shapes = [jax.ShapeDtypeStruct(shape, dtype) for shape, dtype in outs]
    return pl.pallas_call(
        kernel,
        out_shape=shapes if len(shapes) > 1 else shapes[0],
        in_specs=ins,
        out_specs=outputs if len(shapes) > 1 else outputs[0],
        scratch_shapes=list(scratch),
        compiler_params=pltpu.CompilerParams(vmem_limit_bytes=mib << 20),
        cost_estimate=pl.CostEstimate(flops=flops, bytes_accessed=nbytes, transcendentals=0),
        **rest,
    )


def halves(value):
    high = value.astype(jnp.bfloat16)
    low = (value - high.astype(jnp.float32)).astype(jnp.bfloat16)
    return high, low


def dot3(left, right):
    dot = functools.partial(jnp.dot, preferred_element_type=jnp.float32)
    return dot(left[0], right[1]) + dot(left[1], right[0]) + dot(left[0], right[0])


def first_kernel(number, left, right, out, high, low, right_high, right_low):
    columns = pl.ds(pl.multiple_of(number[0] * 256, 256), 256)

    @pl.when(pl.program_id(0) == 0)
    def _():
        right_high[...], right_low[...] = halves(right[:, columns])

    pair = halves(left[...])
    high[...], low[...] = pair
    out[...] = dot3(pair, (right_high[...], right_low[...]))


def second_kernel(number, high, low, right, out, right_high, right_low):
    columns = pl.ds(pl.multiple_of(number[0] * 256, 256), 256)

    @pl.when(pl.program_id(0) == 0)
    def _():
        right_high[...], right_low[...] = halves(right[:, columns])

    out[...] = dot3((high[...], low[...]), (right_high[...], right_low[...]))


def product(number, left, right):
    block = pl.BlockSpec((256, 1024), lambda i: (i, 0))
    out_block = pl.BlockSpec((256, 256), lambda i: (i, 0))
    whole = pl.BlockSpec((1024, 512), lambda i: (0, 0))
    half = pltpu.VMEM((1024, 256), jnp.bfloat16)
    kept = ((1024, 1024), jnp.bfloat16)
    out = ((1024, 256), jnp.float32)
    rest = dict(flops=3 << 29, nbytes=7 << 20, scratch=[half, half], grid=(4,))
    if len(left) == 1:
        outs, specs = [out, kept, kept], [out_block, block, block]
        return call(first_kernel, outs, [SMEM, block, whole], specs, **rest)(number, *left, right)
    return call(second_kernel, [out], [SMEM, block, block, whole], [out_block], **rest)(number, *left, right)


def chunk_kernel(slots, at, pattern, dealt, out):
    for number in range(2):
        mask = pattern[number, at[0]].astype(jnp.float32)
        out[:, number * 256 : number * 256 + 256] = mask * dealt[slots[number]]


def reduce_kernel(at, pattern, terms, column, turned):
    total = terms[0]
    for k in range(1, 8):
        total += terms[k]
    total = -(pattern[at[0], at[1]].astype(jnp.float32) * total)
    column[...] = total
    turned[...] = total.T


def inner_kernel(at, left, right, out):
    rows = pl.ds(pl.multiple_of(at[0] * 128, 128), 128)
    columns = pl.ds(pl.multiple_of(at[1] * 256, 256), 256)
    inner = dot3(halves(left[rows, columns].T), halves(right[...]))
    for k in range(16):
        out[k] = inner[k * 16 : k * 16 + 16]


def rows_kernel(core, mine, other, out):
    for k in range(8):
        columns = slice(k * 128, k * 128 + 128)
        out[core[0], :, columns] = mine[k]
        out[1 - core[0], :, columns] = other[k]


def diag_kernel(given, pieces, out):
    for number in range(2):
        for k in range(16):
            rows = slice(k * 16, k * 16 + 16)
            out[number, rows] = given[number, rows] - pieces[2 * k + number]


def place_kernel(z, *refs):
    *pieces, top, bottom, _, out = refs
    for number in range(2):
        for piece, index in zip(pieces, (0, 7, 6, 5, 1, 2, 3)):
            start = pl.multiple_of(lax.rem(z[0] + index, 8) * 128, 128)
            out[number, pl.ds(start, 128)] = piece[number]
        start = pl.multiple_of(lax.rem(z[0] + 4, 8) * 128, 128)
        out[number, pl.ds(start, 64)] = top[number]
        out[number, pl.ds(start + 64, 64)] = bottom[number]


def both(mine, other, first):
    return jnp.where(first, jnp.stack([mine, other]), jnp.stack([other, mine]))


def ring(block):
    half = block.shape[-2] // 2
    ups, downs = [block], [block]
    for _ in range(3):
        ups.append(lax.ppermute(ups[-1], "z", UP))
        downs.append(lax.ppermute(downs[-1], "z", DOWN))
    top = lax.ppermute(ups[-1][..., :half, :], "z", UP)
    bottom = lax.ppermute(downs[-1][..., half:, :], "z", DOWN)
    return [block] + ups[1:] + downs[1:] + [top, bottom]


def gather_rows(pieces, z):
    out = jnp.zeros((1024, pieces[0].shape[1]), jnp.float32)
    index = [z, z + 7, z + 6, z + 5, z + 1, z + 2, z + 3, z + 4, z + 4]
    for k, piece in enumerate(pieces):
        out = lax.dynamic_update_slice(out, piece, (index[k] % 8 * 128 + (64 if k == 8 else 0), 0))
    return out


def shards(inverse_rows, panels, diag_inverse, pattern, owner_slot):
    row = lax.axis_index(ROW)
    col = lax.axis_index(COL)
    chip = lax.axis_index(CHIP)
    core = lax.axis_index("core")
    z = lax.axis_index("z")
    xh = lax.axis_index("xh")

    dealt = lax.all_to_all(panels[0].reshape(16, 64, 256), COL, 0, 0, tiled=True)
    out = ((64, 512), jnp.float32)
    chunk = call(chunk_kernel, [out], [SMEM] * 3 + [VMEM], [VMEM], nbytes=1 << 18)(
        owner_slot, (row * 4 + col // 4)[None], pattern, dealt
    )
    block = both(chunk, lax.ppermute(chunk, "xh", SWAP), xh == 0).reshape(128, 512)
    masked = gather_rows(ring(block), z)

    sent, *kept = product((1 - core)[None], [inverse_rows], masked)
    received = lax.ppermute(sent, "core", SWAP)
    term = product(core[None], kept, masked) + received
    terms = lax.all_to_all(term.reshape(8, 128, 256), CHIP, 0, 0, tiled=True)
    outs = [((128, 256), jnp.float32), ((256, 128), jnp.float32)]
    at = jnp.stack([core, col * 4 + chip // 2])
    column, turned = call(reduce_kernel, outs, [SMEM, SMEM, VMEM], [VMEM, VMEM])(at, pattern, terms)

    mine = lax.ppermute(column, ALL, TRANSPOSE)
    pieces = ring(both(mine, lax.ppermute(mine, "xh", SWAP), xh == 0))

    out = ((16, 16, 256), jnp.float32)
    at = jnp.stack([z, xh])
    inner = call(inner_kernel, [out], [SMEM, VMEM, VMEM], [VMEM], flops=3 << 24)(at, masked, mine)
    inner = jnp.sum(lax.all_to_all(inner, ROW, 0, 0, tiled=True), axis=0)
    inner = lax.all_to_all(jnp.broadcast_to(inner[None], (8, 16, 256)), "z", 0, 0, tiled=True)
    inner = jnp.sum(inner, axis=0)
    inner = jnp.broadcast_to(inner[None], (32, 16, 256))
    inner = lax.all_to_all(inner, ROW + ("xh",), 0, 0, tiled=True)
    out = ((2, 256, 256), jnp.float32)
    diag = call(diag_kernel, [out], [VMEM, VMEM], [VMEM], nbytes=3 << 19)(diag_inverse, inner)

    turned = jnp.broadcast_to(turned[None], (8, 256, 128))
    turned = lax.all_to_all(turned, CHIP, 0, 0, tiled=True)
    other = lax.ppermute(turned, "core", SWAP)
    out = ((2, 256, 1024), jnp.float32)
    rows = call(rows_kernel, [out], [SMEM, VMEM, VMEM], [VMEM], nbytes=1 << 22)(core[None], turned, other)

    out = ((2, 1024, 256), jnp.float32)
    lower = call(place_kernel, [out], [SMEM] + [VMEM] * 9 + [ANY], [VMEM], nbytes=1 << 22)(
        z[None], *pieces, rows
    )
    return lower, rows, diag


def solution(mesh):
    fine = Mesh(np.asarray(mesh.devices).reshape(4, 2, 2, 8, 2), ALL)
    in_specs = (P(COL, ROW), P(COL, ROW, None), P(), P(), P())
    out_specs = (P(None, ROW, None), P(None, None, COL), P())
    return jax.shard_map(shards, mesh=fine, in_specs=in_specs, out_specs=out_specs, check_vma=False)
```

```python
import functools

import jax
import jax.numpy as jnp
import numpy as np
from jax import lax
from jax.experimental import pallas as pl
from jax.experimental.pallas import tpu as pltpu
from jax.sharding import Mesh
from jax.sharding import PartitionSpec as P

ROW = ("y", "xl", "core")
CHIP = ("y", "xl")
COL = ("z", "xh")
ALL = ROW + COL
SMEM = pl.BlockSpec(memory_space=pltpu.SMEM)
VMEM = pl.BlockSpec(memory_space=pltpu.VMEM)
ANY = pl.BlockSpec(memory_space=pl.ANY)
SWAP = [(0, 1), (1, 0)]
TRANSPOSE = [(r * 16 + c, c * 16 + r) for r in range(16) for c in range(16)]
UP = [(i, (i + 1) % 8) for i in range(8)]
DOWN = [(i, (i - 1) % 8) for i in range(8)]


def call(kernel, outs, ins, outputs, flops=0, nbytes=1 << 21, scratch=(), mib=24, **rest):
    shapes = [jax.ShapeDtypeStruct(shape, dtype) for shape, dtype in outs]
    return pl.pallas_call(
        kernel,
        out_shape=shapes if len(shapes) > 1 else shapes[0],
        in_specs=ins,
        out_specs=outputs if len(shapes) > 1 else outputs[0],
        scratch_shapes=list(scratch),
        compiler_params=pltpu.CompilerParams(vmem_limit_bytes=mib << 20),
        cost_estimate=pl.CostEstimate(flops=flops, bytes_accessed=nbytes, transcendentals=0),
        **rest,
    )


def halves(value):
    high = value.astype(jnp.bfloat16)
    low = (value - high.astype(jnp.float32)).astype(jnp.bfloat16)
    return high, low


def dot3(left, right):
    dot = functools.partial(jnp.dot, preferred_element_type=jnp.float32)
    return dot(left[0], right[1]) + dot(left[1], right[0]) + dot(left[0], right[0])


def first_kernel(number, left, right, out, high, low, right_high, right_low):
    columns = pl.ds(pl.multiple_of(number[0] * 256, 256), 256)

    @pl.when(pl.program_id(0) == 0)
    def _():
        right_high[...], right_low[...] = halves(right[:, columns])

    pair = halves(left[...])
    high[...], low[...] = pair
    out[...] = dot3(pair, (right_high[...], right_low[...]))


def second_kernel(number, high, low, right, out, right_high, right_low):
    columns = pl.ds(pl.multiple_of(number[0] * 256, 256), 256)

    @pl.when(pl.program_id(0) == 0)
    def _():
        right_high[...], right_low[...] = halves(right[:, columns])

    out[...] = dot3((high[...], low[...]), (right_high[...], right_low[...]))


def product(number, left, right):
    block = pl.BlockSpec((256, 1024), lambda i: (i, 0))
    out_block = pl.BlockSpec((256, 256), lambda i: (i, 0))
    whole = pl.BlockSpec((1024, 512), lambda i: (0, 0))
    half = pltpu.VMEM((1024, 256), jnp.bfloat16)
    kept = ((1024, 1024), jnp.bfloat16)
    out = ((1024, 256), jnp.float32)
    rest = dict(flops=3 << 29, nbytes=7 << 20, scratch=[half, half], grid=(4,))
    if len(left) == 1:
        outs, specs = [out, kept, kept], [out_block, block, block]
        return call(first_kernel, outs, [SMEM, block, whole], specs, **rest)(number, *left, right)
    return call(second_kernel, [out], [SMEM, block, block, whole], [out_block], **rest)(number, *left, right)


def chunk_kernel(slots, at, pattern, dealt, out):
    for number in range(2):
        mask = pattern[number, at[0]].astype(jnp.float32)
        out[:, number * 256 : number * 256 + 256] = mask * dealt[slots[number]]


def reduce_kernel(at, pattern, terms, column, turned):
    total = terms[0]
    for k in range(1, 8):
        total += terms[k]
    total = -(pattern[at[0], at[1]].astype(jnp.float32) * total)
    column[...] = total
    turned[...] = total.T


def inner_kernel(at, left, right, out):
    columns = pl.ds(pl.multiple_of(at[0] * 256, 256), 256)
    inner = dot3(halves(left[:, columns].T), halves(right[...]))
    for k in range(16):
        out[k] = inner[k * 16 : k * 16 + 16]


def rows_kernel(core, mine, other, out, done):
    for k in range(8):
        columns = slice(k * 128, k * 128 + 128)
        out[core[0], :, columns] = mine[k]
        out[1 - core[0], :, columns] = other[k]
    done[...] = mine[0, :8]


def add_kernel(pieces, out):
    total = pieces[0]
    for k in range(1, pieces.shape[0]):
        total += pieces[k]
    for k in range(out.shape[0]):
        out[k] = total


def add_up(pieces, receivers):
    out = ((receivers, 16, 256), jnp.float32)
    return call(add_kernel, [out], [VMEM], [VMEM], nbytes=1 << 19)(pieces)


def pair_kernel(xh, mine, other, out):
    out[xh[0]] = mine[...]
    out[1 - xh[0]] = other[...]


def diag_kernel(given, pieces, out):
    for number in range(2):
        for k in range(16):
            rows = slice(k * 16, k * 16 + 16)
            out[number, rows] = given[number, rows] - pieces[2 * k + number]


def place_kernel(z, *refs):
    *pieces, top, bottom, _, out = refs
    for number in range(2):
        for piece, index in zip(pieces, (0, 7, 6, 5, 1, 2, 3)):
            start = pl.multiple_of(lax.rem(z[0] + index, 8) * 128, 128)
            out[number, pl.ds(start, 128)] = piece[number]
        start = pl.multiple_of(lax.rem(z[0] + 4, 8) * 128, 128)
        out[number, pl.ds(start, 64)] = top[number]
        out[number, pl.ds(start + 64, 64)] = bottom[number]


def both(mine, other, first):
    return jnp.where(first, jnp.stack([mine, other]), jnp.stack([other, mine]))


def ring(block):
    half = block.shape[-2] // 2
    ups, downs = [block], [block]
    for _ in range(3):
        ups.append(lax.ppermute(ups[-1], "z", UP))
        downs.append(lax.ppermute(downs[-1], "z", DOWN))
    top = lax.ppermute(ups[-1][..., :half, :], "z", UP)
    bottom = lax.ppermute(downs[-1][..., half:, :], "z", DOWN)
    return [block] + ups[1:] + downs[1:] + [top, bottom]


def gather_rows(pieces, z):
    out = jnp.zeros((1024, pieces[0].shape[1]), jnp.float32)
    index = [z, z + 7, z + 6, z + 5, z + 1, z + 2, z + 3, z + 4, z + 4]
    for k, piece in enumerate(pieces):
        out = lax.dynamic_update_slice(out, piece, (index[k] % 8 * 128 + (64 if k == 8 else 0), 0))
    return out


def shards(inverse_rows, panels, diag_inverse, pattern, owner_slot):
    row = lax.axis_index(ROW)
    col = lax.axis_index(COL)
    chip = lax.axis_index(CHIP)
    core = lax.axis_index("core")
    z = lax.axis_index("z")
    xh = lax.axis_index("xh")

    dealt = lax.all_to_all(panels[0].reshape(16, 64, 256), COL, 0, 0, tiled=True)
    out = ((64, 512), jnp.float32)
    chunk = call(chunk_kernel, [out], [SMEM] * 3 + [VMEM], [VMEM], nbytes=1 << 18)(
        owner_slot, (row * 4 + col // 4)[None], pattern, dealt
    )
    block = both(chunk, lax.ppermute(chunk, "xh", SWAP), xh == 0).reshape(128, 512)
    masked = gather_rows(ring(block), z)

    sent, *kept = product((1 - core)[None], [inverse_rows], masked)
    received = lax.ppermute(sent, "core", SWAP)
    term = product(core[None], kept, masked) + received
    terms = lax.all_to_all(term.reshape(8, 128, 256), CHIP, 0, 0, tiled=True)
    outs = [((128, 256), jnp.float32), ((256, 128), jnp.float32)]
    at = jnp.stack([core, col * 4 + chip // 2])
    column, turned = call(reduce_kernel, outs, [SMEM, SMEM, VMEM], [VMEM, VMEM])(at, pattern, terms)

    mine = lax.ppermute(column, ALL, TRANSPOSE)
    other = lax.ppermute(mine, "xh", SWAP)
    out = ((2, 128, 256), jnp.float32)
    pieces = ring(call(pair_kernel, [out], [SMEM, VMEM, VMEM], [VMEM], nbytes=1 << 19)(xh[None], mine, other))

    out = ((16, 16, 256), jnp.float32)
    inner = call(inner_kernel, [out], [SMEM, VMEM, VMEM], [VMEM], flops=3 << 24)(xh[None], block, mine)
    inner = add_up(lax.all_to_all(inner, ROW, 0, 0, tiled=True), 8)
    inner = add_up(lax.all_to_all(inner, "z", 0, 0, tiled=True), 32)
    inner = lax.all_to_all(inner, ROW + ("xh",), 0, 0, tiled=True)
    out = ((2, 256, 256), jnp.float32)
    diag = call(diag_kernel, [out], [VMEM, VMEM], [VMEM], nbytes=3 << 19)(diag_inverse, inner)

    turned = jnp.broadcast_to(turned[None], (8, 256, 128))
    turned = lax.all_to_all(turned, CHIP, 0, 0, tiled=True)
    other = lax.ppermute(turned, "core", SWAP)
    outs = [((2, 256, 1024), jnp.float32), ((8, 128), jnp.float32)]
    rows, done = call(rows_kernel, outs, [SMEM, VMEM, VMEM], [VMEM] * 2, nbytes=1 << 22)(core[None], turned, other)

    out = ((2, 1024, 256), jnp.float32)
    lower = call(place_kernel, [out], [SMEM] + [VMEM] * 9 + [ANY], [VMEM], nbytes=1 << 22)(
        z[None], *pieces, done
    )
    return lower, rows, diag


def solution(mesh):
    fine = Mesh(np.asarray(mesh.devices).reshape(4, 2, 2, 8, 2), ALL)
    in_specs = (P(COL, ROW), P(COL, ROW, None), P(), P(), P())
    out_specs = (P(None, ROW, None), P(None, None, COL), P())
    return jax.shard_map(shards, mesh=fine, in_specs=in_specs, out_specs=out_specs, check_vma=False)
```

```python
import functools

import jax
import jax.numpy as jnp
import numpy as np
from jax import lax
from jax.experimental import pallas as pl
from jax.experimental.pallas import tpu as pltpu
from jax.sharding import Mesh
from jax.sharding import PartitionSpec as P

ROW = ("y", "xl", "core")
CHIP = ("y", "xl")
COL = ("z", "xh")
ALL = ROW + COL
SMEM = pl.BlockSpec(memory_space=pltpu.SMEM)
VMEM = pl.BlockSpec(memory_space=pltpu.VMEM)
ANY = pl.BlockSpec(memory_space=pl.ANY)
SWAP = [(0, 1), (1, 0)]
TRANSPOSE = [(r * 16 + c, c * 16 + r) for r in range(16) for c in range(16)]
UP = [(i, (i + 1) % 8) for i in range(8)]
DOWN = [(i, (i - 1) % 8) for i in range(8)]


def call(kernel, outs, ins, outputs, flops=0, nbytes=1 << 21, scratch=(), mib=24, **rest):
    shapes = [jax.ShapeDtypeStruct(shape, dtype) for shape, dtype in outs]
    return pl.pallas_call(
        kernel,
        out_shape=shapes if len(shapes) > 1 else shapes[0],
        in_specs=ins,
        out_specs=outputs if len(shapes) > 1 else outputs[0],
        scratch_shapes=list(scratch),
        compiler_params=pltpu.CompilerParams(vmem_limit_bytes=mib << 20),
        cost_estimate=pl.CostEstimate(flops=flops, bytes_accessed=nbytes, transcendentals=0),
        **rest,
    )


def halves(value):
    high = value.astype(jnp.bfloat16)
    low = (value - high.astype(jnp.float32)).astype(jnp.bfloat16)
    return high, low


def dot3(left, right):
    dot = functools.partial(jnp.dot, preferred_element_type=jnp.float32)
    return dot(left[0], right[1]) + dot(left[1], right[0]) + dot(left[0], right[0])


def first_kernel(number, left, right, out, high, low, right_high, right_low):
    columns = pl.ds(pl.multiple_of(number[0] * 256, 256), 256)

    @pl.when(pl.program_id(0) == 0)
    def _():
        right_high[...], right_low[...] = halves(right[:, columns])

    pair = halves(left[...])
    high[...], low[...] = pair
    out[...] = dot3(pair, (right_high[...], right_low[...]))


def second_kernel(number, high, low, right, out, right_high, right_low):
    columns = pl.ds(pl.multiple_of(number[0] * 256, 256), 256)

    @pl.when(pl.program_id(0) == 0)
    def _():
        right_high[...], right_low[...] = halves(right[:, columns])

    out[...] = dot3((high[...], low[...]), (right_high[...], right_low[...]))


def product(number, left, right):
    block = pl.BlockSpec((256, 1024), lambda i: (i, 0))
    out_block = pl.BlockSpec((256, 256), lambda i: (i, 0))
    whole = pl.BlockSpec((1024, 512), lambda i: (0, 0))
    half = pltpu.VMEM((1024, 256), jnp.bfloat16)
    kept = ((1024, 1024), jnp.bfloat16)
    out = ((1024, 256), jnp.float32)
    rest = dict(flops=3 << 29, nbytes=7 << 20, scratch=[half, half], grid=(4,))
    if len(left) == 1:
        outs, specs = [out, kept, kept], [out_block, block, block]
        return call(first_kernel, outs, [SMEM, block, whole], specs, **rest)(number, *left, right)
    return call(second_kernel, [out], [SMEM, block, block, whole], [out_block], **rest)(number, *left, right)


def last_kernel(at, high, low, top, bottom, term, *rest):
    *more, out = rest
    depth = pl.ds(pl.multiple_of(at[0] * 128, 128), 128)
    columns = pl.ds(pl.multiple_of(at[1] * 256, 256), 256)
    right = halves(jnp.concatenate([top[:, columns], bottom[:, columns]]))
    for k in range(4):
        rows = slice(k * 256, k * 256 + 256)
        total = term[rows] + dot3((high[rows, depth], low[rows, depth]), right)
        out[rows] = total + more[0][rows] if more else total


def add_last(at, kept, top, bottom, *terms):
    out = ((1024, 256), jnp.float32)
    return call(last_kernel, [out], [SMEM] + [VMEM] * (4 + len(terms)), [VMEM], flops=3 << 26)(
        at, *kept, top, bottom, *terms
    )


def chunk_kernel(slots, at, pattern, dealt, out):
    for number in range(2):
        mask = pattern[number, at[0]].astype(jnp.float32)
        out[:, number * 256 : number * 256 + 256] = mask * dealt[slots[number]]


def reduce_kernel(at, pattern, terms, column, turned):
    total = terms[0]
    for k in range(1, 8):
        total += terms[k]
    total = -(pattern[at[0], at[1]].astype(jnp.float32) * total)
    column[...] = total
    turned[...] = total.T


def inner_kernel(at, left, right, out):
    columns = pl.ds(pl.multiple_of(at[0] * 256, 256), 256)
    inner = dot3(halves(left[:, columns].T), halves(right[...]))
    for k in range(16):
        out[k] = inner[k * 16 : k * 16 + 16]


def rows_kernel(core, mine, other, out, done):
    for k in range(8):
        columns = slice(k * 128, k * 128 + 128)
        out[core[0], :, columns] = mine[k]
        out[1 - core[0], :, columns] = other[k]
    done[...] = mine[0, :8]


def add_kernel(pieces, out):
    total = pieces[0]
    for k in range(1, pieces.shape[0]):
        total += pieces[k]
    for k in range(out.shape[0]):
        out[k] = total


def add_up(pieces, receivers):
    out = ((receivers, 16, 256), jnp.float32)
    return call(add_kernel, [out], [VMEM], [VMEM], nbytes=1 << 19)(pieces)


def pair_kernel(xh, mine, other, out):
    out[xh[0]] = mine[...]
    out[1 - xh[0]] = other[...]


def diag_kernel(given, pieces, out):
    for number in range(2):
        for k in range(16):
            rows = slice(k * 16, k * 16 + 16)
            out[number, rows] = given[number, rows] - pieces[2 * k + number]


def place_kernel(z, *refs):
    *pieces, top, bottom, _, out = refs
    for number in range(2):
        for piece, index in zip(pieces, (0, 7, 6, 5, 1, 2, 3)):
            start = pl.multiple_of(lax.rem(z[0] + index, 8) * 128, 128)
            out[number, pl.ds(start, 128)] = piece[number]
        start = pl.multiple_of(lax.rem(z[0] + 4, 8) * 128, 128)
        out[number, pl.ds(start, 64)] = top[number]
        out[number, pl.ds(start + 64, 64)] = bottom[number]


def both(mine, other, first):
    return jnp.where(first, jnp.stack([mine, other]), jnp.stack([other, mine]))


def ring(block):
    half = block.shape[-2] // 2
    ups, downs = [block], [block]
    for _ in range(3):
        ups.append(lax.ppermute(ups[-1], "z", UP))
        downs.append(lax.ppermute(downs[-1], "z", DOWN))
    top = lax.ppermute(ups[-1][..., :half, :], "z", UP)
    bottom = lax.ppermute(downs[-1][..., half:, :], "z", DOWN)
    return [block] + ups[1:] + downs[1:] + [top, bottom]


def gather_rows(pieces, z):
    out = jnp.zeros((1024, pieces[0].shape[1]), jnp.float32)
    index = [z, z + 7, z + 6, z + 5, z + 1, z + 2, z + 3, z + 4, z + 4]
    for k, piece in enumerate(pieces):
        out = lax.dynamic_update_slice(out, piece, (index[k] % 8 * 128 + (64 if k == 8 else 0), 0))
    return out


def shards(inverse_rows, panels, diag_inverse, pattern, owner_slot):
    row = lax.axis_index(ROW)
    col = lax.axis_index(COL)
    chip = lax.axis_index(CHIP)
    core = lax.axis_index("core")
    z = lax.axis_index("z")
    xh = lax.axis_index("xh")

    dealt = lax.all_to_all(panels[0].reshape(16, 64, 256), COL, 0, 0, tiled=True)
    out = ((64, 512), jnp.float32)
    chunk = call(chunk_kernel, [out], [SMEM] * 3 + [VMEM], [VMEM], nbytes=1 << 18)(
        owner_slot, (row * 4 + col // 4)[None], pattern, dealt
    )
    block = both(chunk, lax.ppermute(chunk, "xh", SWAP), xh == 0).reshape(128, 512)
    *came, top, bottom = ring(block)
    masked = gather_rows(came, z)

    sent, *kept = product((1 - core)[None], [inverse_rows], masked)
    term = product(core[None], kept, masked)
    sent = add_last(jnp.stack([(z + 4) % 8, 1 - core]), kept, top, bottom, sent)
    received = lax.ppermute(sent, "core", SWAP)
    term = add_last(jnp.stack([(z + 4) % 8, core]), kept, top, bottom, term, received)
    terms = lax.all_to_all(term.reshape(8, 128, 256), CHIP, 0, 0, tiled=True)
    outs = [((128, 256), jnp.float32), ((256, 128), jnp.float32)]
    at = jnp.stack([core, col * 4 + chip // 2])
    column, turned = call(reduce_kernel, outs, [SMEM, SMEM, VMEM], [VMEM, VMEM])(at, pattern, terms)

    mine = lax.ppermute(column, ALL, TRANSPOSE)
    other = lax.ppermute(mine, "xh", SWAP)
    out = ((2, 128, 256), jnp.float32)
    pieces = ring(call(pair_kernel, [out], [SMEM, VMEM, VMEM], [VMEM], nbytes=1 << 19)(xh[None], mine, other))

    out = ((16, 16, 256), jnp.float32)
    inner = call(inner_kernel, [out], [SMEM, VMEM, VMEM], [VMEM], flops=3 << 24)(xh[None], block, mine)
    inner = add_up(lax.all_to_all(inner, ROW, 0, 0, tiled=True), 8)
    inner = add_up(lax.all_to_all(inner, "z", 0, 0, tiled=True), 32)
    inner = lax.all_to_all(inner, ROW + ("xh",), 0, 0, tiled=True)
    out = ((2, 256, 256), jnp.float32)
    diag = call(diag_kernel, [out], [VMEM, VMEM], [VMEM], nbytes=3 << 19)(diag_inverse, inner)

    turned = jnp.broadcast_to(turned[None], (8, 256, 128))
    turned = lax.all_to_all(turned, CHIP, 0, 0, tiled=True)
    other = lax.ppermute(turned, "core", SWAP)
    outs = [((2, 256, 1024), jnp.float32), ((8, 128), jnp.float32)]
    rows, done = call(rows_kernel, outs, [SMEM, VMEM, VMEM], [VMEM] * 2, nbytes=1 << 22)(core[None], turned, other)

    out = ((2, 1024, 256), jnp.float32)
    lower = call(place_kernel, [out], [SMEM] + [VMEM] * 9 + [ANY], [VMEM], nbytes=1 << 22)(
        z[None], *pieces, done
    )
    return lower, rows, diag


def solution(mesh):
    fine = Mesh(np.asarray(mesh.devices).reshape(4, 2, 2, 8, 2), ALL)
    in_specs = (P(COL, ROW), P(COL, ROW, None), P(), P(), P())
    out_specs = (P(None, ROW, None), P(None, None, COL), P())
    return jax.shard_map(shards, mesh=fine, in_specs=in_specs, out_specs=out_specs, check_vma=False)
```
